32 devices in a mesh: gx: 8 (over z, x), gy: 4 (over y, core).
Axes of the slice: x: 2, y: 2, z: 4, core: 2. Of those that a mesh axis runs over, the one named last changes fastest.
Arguments:
- innovations: float32 [2, 128, 16384], P(None, None, ('gx', 'gy')), may hold values from -18 to 18
- obs_column: int32 [16384], P(('gx', 'gy')), may hold values from 0 to 16383
- obs_scale: float32 [2, 128], replicated, may hold values from 0.25 to 4
- band_of_lat: int32 [512], P('gy'), may hold values from 0 to 7, as said below
- balance: bfloat16 [8, 2, 128, 128], replicated, may hold values from -0.3 to 1.5
- lon_filter: bfloat16 [2, 1024, 1024], replicated, may hold values from 0 to 1
- lat_filter: bfloat16 [2, 512, 512], replicated, may hold values from 0 to 1
Outputs:
- control: float32 [2, 128, 1024, 512], P(None, ('gx', 'gy'))
- increment: float32 [2, 128, 1024, 512], P(None, None, 'gx', 'gy')
The draws below stay inside these ranges and needn't reach their ends.
Inputs may be any that keep to these rules, and one draw needn't show every extreme that they name: `obs_column`: column c of a tile lies at longitude offset c // 128 and latitude offset c % 128 within the tile. `band_of_lat`: never falls from one latitude to the next.
All inputs are finite; a program needn't handle non-finite values.
Results may differ from the reference program's by a relative error of at most 0.0049.
Values may be sent and summed in bfloat16 or wider, within the bound.
A program may use at most 192 MiB of HBM per device.

```python
import math
import jax
import jax.numpy as jnp
from jax import lax

NLON = 1024
NLAT = 512
NLEV = 128
NVAR = 2
NBAND = 8
OBS_DEV = 512
ITERS = 2
LON_T = 128
LAT_T = 128
COLS_T = 16384
NOBS = 16384
N_GY = 4


def draw_innovations(key, part):
    key_main = jax.random.fold_in(key, 0)
    tile_index = jnp.arange(NOBS, dtype=jnp.int32) // OBS_DEV
    growth = 1.0 + 2.0 * tile_index.astype(jnp.float32) / max(NOBS // OBS_DEV - 1, 1)
    values = jax.random.normal(key_main, (NVAR, NLEV, NOBS), jnp.float32)
    return (jnp.clip(values, -6.0, 6.0) * growth[None, None, :]).astype(jnp.float32)


def draw_obs_scale(key, part):
    level_pos = jnp.arange(NLEV, dtype=jnp.float32) / max(NLEV - 1, 1)
    noise = jax.random.uniform(key, (NVAR, NLEV), jnp.float32, -0.3, 0.3)
    return (0.6 * jnp.exp(noise) * jnp.power(3.0, level_pos)[None, :]).astype(jnp.float32)


def draw_band_of_lat(key, part):
    jitter = NLAT // (4 * NBAND)
    bounds = jnp.arange(1, NBAND, dtype=jnp.int32) * NLAT // NBAND
    bounds = bounds + jax.random.randint(key, (NBAND - 1,), -jitter, jitter + 1, dtype=jnp.int32)
    rows = jnp.arange(NLAT, dtype=jnp.int32)
    return jnp.sum((rows[:, None] >= bounds[None, :]).astype(jnp.int32), axis=1).astype(jnp.int32)


def draw_balance(key, part):
    key_diag, key_off = jax.random.split(key)
    diagonal = jax.random.uniform(key_diag, (NBAND, NVAR, NLEV, 1), jnp.float32, 0.8, 1.2)
    rows = jnp.arange(NLEV, dtype=jnp.int32)
    identity = (rows[:, None] == rows[None, :]).astype(jnp.float32)
    offdiag = jnp.clip(jax.random.normal(key_off, (NBAND, NVAR, NLEV, NLEV), jnp.float32), -5.0, 5.0)
    offdiag = offdiag * (0.6 / math.sqrt(NLEV))
    return (identity * diagonal + offdiag).astype(jnp.bfloat16)


def line_filter(key, length, periodic):
    rows = jnp.arange(length, dtype=jnp.float32)
    distance = jnp.abs(rows[:, None] - rows[None, :])
    if periodic:
        distance = jnp.minimum(distance, length - distance)
    kernel = jnp.zeros((length, length), jnp.float32)
    for weight_part, width_part in ((0.5, 2.0), (0.3, max(length / 32.0, 1.0)), (0.2, max(length / 6.0, 1.0))):
        kernel = kernel + weight_part * jnp.exp(-distance * distance / (2.0 * width_part * width_part)) / (math.sqrt(2.0 * math.pi) * width_part)
    identity = (rows[:, None] == rows[None, :]).astype(jnp.float32)
    factor = jax.random.uniform(key, (NVAR, length, length), jnp.float32, 0.5, 1.5)
    return ((0.3 * identity + 0.7 * kernel)[None, :, :] * factor).astype(jnp.bfloat16)


def draw_lon_filter(key, part):
    return line_filter(key, NLON, True)


def draw_lat_filter(key, part):
    return line_filter(key, NLAT, False)


def place_ends(values, stream_key, low, high):
    place = [jax.random.randint(jax.random.fold_in(stream_key, axis), (), 0, length) for axis, length in enumerate(values.shape)]
    widest = values.shape.index(max(values.shape))
    next_to = place[:widest] + [(place[widest] + 1) % values.shape[widest]] + place[widest + 1:]
    return values.at[tuple(place)].set(low).at[tuple(next_to)].set(high)


def setup_inputs(seed: int = 0) -> dict:
    keys = jax.random.split(jax.random.key(seed), 8)
    return {
        "innovations": draw_innovations(jax.random.fold_in(keys[7], 71), 0),
        "obs_column": place_ends(jax.random.randint(keys[1], (NOBS,), 0, COLS_T), jax.random.fold_in(keys[1], 1), 0, COLS_T - 1).astype(jnp.int32),
        "obs_scale": draw_obs_scale(jax.random.fold_in(keys[7], 71), 0),
        "band_of_lat": draw_band_of_lat(jax.random.fold_in(keys[7], 71), 0),
        "balance": draw_balance(jax.random.fold_in(keys[7], 71), 0),
        "lon_filter": draw_lon_filter(jax.random.fold_in(keys[7], 71), 0),
        "lat_filter": draw_lat_filter(jax.random.fold_in(keys[7], 71), 0),
    }


huber_edge = 1.5


def rounded(value):
    return lax.optimization_barrier(value.astype(jnp.bfloat16)).astype(jnp.float32)


def reference(innovations, obs_column, obs_scale, band_of_lat, balance, lon_filter, lat_filter):
    tile_index = jnp.arange(NOBS, dtype=jnp.int32) // OBS_DEV
    lon_index = (tile_index // N_GY) * LON_T + obs_column // LAT_T
    lat_index = (tile_index % N_GY) * LAT_T + obs_column % LAT_T
    obs_site = (lon_index * NLAT + lat_index).astype(jnp.int32)
    balance_lat = balance[band_of_lat].astype(jnp.float32)
    lon_wide = lon_filter.astype(jnp.float32)
    lat_wide = lat_filter.astype(jnp.float32)
    inv_scale = obs_scale[:, :, None]
    grid_shape = (NVAR, NLEV, NLON, NLAT)
    control = jnp.zeros(grid_shape, jnp.float32)
    increment = jnp.zeros((NVAR, NLEV, NLON * NLAT), jnp.float32)
    for iteration in range(ITERS):
        observed = increment[:, :, obs_site]
        scaled = (observed - innovations) * inv_scale
        weighted = jnp.clip(scaled, -huber_edge, huber_edge) * inv_scale
        forcing = jnp.zeros((NVAR, NLEV, NLON * NLAT), jnp.float32).at[:, :, obs_site].add(weighted)
        forcing = rounded(forcing).reshape(grid_shape)
        balanced = rounded(jnp.einsum("tvlm,vlxt->vmxt", balance_lat, forcing))
        half_lon = rounded(jnp.einsum("vij,vlik->vljk", lon_wide, balanced))
        adjoint = jnp.einsum("vljm,vmk->vljk", half_lon, lat_wide)
        gradient = control + adjoint
        grad_norm = jnp.sum(gradient * gradient)
        grad_round = rounded(gradient)
        smooth_lon = rounded(jnp.einsum("vij,vljk->vlik", lon_wide, grad_round))
        smoothed = rounded(jnp.einsum("vlim,vkm->vlik", smooth_lon, lat_wide))
        response = jnp.einsum("tvlm,vmxt->vlxt", balance_lat, smoothed).reshape(NVAR, NLEV, NLON * NLAT)
        at_obs = response[:, :, obs_site]
        weight = huber_edge / jnp.maximum(jnp.abs(scaled), huber_edge)
        curvature = jnp.sum(weight * (inv_scale * at_obs) ** 2)
        step_size = grad_norm / (grad_norm + curvature)
        control = control - step_size * gradient
        increment = increment - step_size * response
    return control, increment.reshape(grid_shape)
```

```python
import jax
import jax.numpy as jnp
from jax import lax
from jax.sharding import PartitionSpec as P

ITERS = 2


huber_edge = 1.5
AXES = ("gx", "gy")
f32 = jnp.float32
bf16 = jnp.bfloat16


def shards(innovations, obs_column, obs_scale, band_of_lat, balance, lon_filter, lat_filter):
    lon_parts = lax.axis_size("gx")
    lat_parts = lax.axis_size("gy")
    devices = lon_parts * lat_parts
    var_count, levels, obs_count = innovations.shape
    bands = balance.shape[0]
    lon_full = lon_filter.shape[1]
    lat_full = lat_filter.shape[1]
    lon_tile = lon_full // lon_parts
    lat_tile = lat_full // lat_parts
    per_dev = levels // devices
    lon_tiled = lon_filter.reshape(var_count, lon_parts, lon_tile, lon_full)
    lat_tiled = lat_filter.reshape(var_count, lat_parts, lat_tile, lat_full)
    inv_scale = obs_scale[:, :, None]
    band_ids = jnp.arange(bands, dtype=jnp.int32)
    band_hot = (band_of_lat[:, None] == band_ids[None, :]).astype(bf16)
    balance_lat = jnp.einsum("tb,bvlm->tvlm", band_hot, balance, preferred_element_type=f32).astype(
        bf16
    )

    own_lat = obs_column % lat_tile
    own_hot = own_lat[:, None] == jnp.arange(lat_tile, dtype=jnp.int32)[None, :]
    own_band = jnp.sum(jnp.where(own_hot, band_of_lat[None, :], 0), axis=1)
    in_band = (own_band[None, :] == band_ids[:, None]).astype(bf16)
    same = obs_column[:, None] == obs_column[None, :]
    order = jnp.arange(obs_count, dtype=jnp.int32)
    first = jnp.logical_not(jnp.any(same & (order[None, :] < order[:, None]), axis=1))
    same = same.astype(f32)

    sites = lax.all_gather(obs_column, AXES, tiled=True).reshape(lon_parts, lat_parts, obs_count)
    hot_lon = (
        (sites // lat_tile)[..., None] == jnp.arange(lon_tile, dtype=jnp.int32)
    ).astype(bf16)
    hot_lat = ((sites % lat_tile)[..., None] == jnp.arange(lat_tile, dtype=jnp.int32)).astype(bf16)

    def to_levels(values):
        return lax.all_to_all(
            values.reshape(var_count, devices, per_dev, -1), AXES, 1, 1, tiled=True
        )

    control = None
    total = None
    at_obs = None
    step_size = None
    for iteration in range(ITERS):
        if iteration == 0:
            observed = jnp.zeros_like(innovations)
        elif iteration == 1:
            observed = -step_size * at_obs
        else:
            observed = observed - step_size * at_obs
        scaled = (observed - innovations) * inv_scale
        weighted = jnp.clip(scaled, -huber_edge, huber_edge) * inv_scale
        forcing = jnp.einsum(
            "vlj,jk->vlk", weighted, same, precision=lax.Precision.HIGHEST
        ).astype(bf16)
        banded = forcing[None] * in_band[:, None, None, :]
        balanced = jnp.einsum("bvlm,bvlj->vmj", balance, banded, preferred_element_type=f32)
        balanced = jnp.where(first, balanced, 0.0).astype(bf16)
        pieces = to_levels(balanced).reshape(var_count, lon_parts, lat_parts, per_dev, obs_count)
        spread = jnp.einsum("vablj->abjvl", pieces)[..., None] * hot_lat[:, :, :, None, None, :]
        grid = jnp.einsum("abjx,abjvlt->abxvlt", hot_lon, spread, preferred_element_type=f32).astype(
            bf16
        )
        half_lon = jnp.einsum(
            "vaxj,abxvlt->vbljt", lon_tiled, grid, preferred_element_type=f32
        ).astype(bf16)
        adjoint = jnp.einsum("vbljt,vbtk->vljk", half_lon, lat_tiled, preferred_element_type=f32)
        gradient = adjoint if control is None else control + adjoint
        grad_local = jnp.sum(gradient * gradient)
        smooth_lon = jnp.einsum(
            "vaxj,vljk->vlaxk", lon_tiled, gradient.astype(bf16), preferred_element_type=f32
        ).astype(bf16)
        smoothed = jnp.einsum(
            "vlaxm,vbtm->vablxt", smooth_lon, lat_tiled, preferred_element_type=f32
        ).astype(bf16)
        rows = jnp.einsum("abjx,vablxt->abjvlt", hot_lon, smoothed, preferred_element_type=f32)
        rows = rows.astype(bf16) * hot_lat[:, :, :, None, None, :]
        picked = jnp.sum(rows.astype(f32), axis=-1).astype(bf16)
        picked = jnp.einsum("abjvl->vablj", picked).reshape(var_count, devices, per_dev, obs_count)
        seen = lax.all_to_all(picked, AXES, 1, 1, tiled=True)
        seen = seen.reshape(var_count, levels, obs_count)
        seen = seen[None] * in_band[:, None, None, :]
        at_obs = jnp.einsum("bvlm,bvmj->vlj", balance, seen, preferred_element_type=f32)
        weight = huber_edge / jnp.maximum(jnp.abs(scaled), huber_edge)
        curve_local = jnp.sum(weight * (inv_scale * at_obs) ** 2)
        sums = lax.psum(jnp.stack([grad_local, curve_local]), AXES)
        grad_norm = sums[0]
        step_size = grad_norm / (grad_norm + sums[1])
        moved = -step_size * gradient
        control = moved if control is None else control + moved
        moved = -step_size * smoothed.astype(f32)
        total = moved if total is None else total + moved
    outgoing = total.astype(bf16).reshape(var_count, devices, per_dev, lon_tile, lat_tile)
    returned = lax.all_to_all(outgoing, AXES, split_axis=1, concat_axis=1, tiled=True)
    returned = returned.reshape(var_count, levels, lon_tile, lat_tile)
    increment = jnp.einsum("tvlm,vmxt->vlxt", balance_lat, returned, preferred_element_type=f32)
    return (control, increment)


def solution(mesh):
    in_specs = (P(None, None, AXES), P(AXES), P(), P("gy"), P(), P(), P())
    out_specs = (P(None, AXES, None, None), P(None, None, "gx", "gy"))
    return jax.shard_map(shards, mesh=mesh, in_specs=in_specs, out_specs=out_specs, check_vma=False)
```
